256 devices in a mesh: dp: 16 (over y, x), ctx: 16 (over z, core).
Axes of the slice: x: 4, y: 4, z: 8, core: 2. Of those that a mesh axis runs over, the one named last changes fastest.
Arguments:
- frames: bfloat16 [8192, 6144], P('ctx'), may hold values from -6 to 6
- proj_weight: bfloat16 [3, 6144, 4096], P(None, 'ctx', 'dp'), may hold values from -0.078125 to 0.078125
- out_weight: bfloat16 [6144, 4096], P('dp', 'ctx'), may hold values from -0.09375 to 0.09375
- query_gain: float32 [4096], P('dp'), may hold values from 0.5 to 2
- key_gain: float32 [4096], P('dp'), may hold values from 0.5 to 2
- key_tiles: int32 [32, 128, 18], P('dp', 'ctx'), may hold values from 0 to 127, as said below
- key_counts: int32 [32, 128], P('dp', 'ctx'), may hold values from 1 to 18
Outputs:
- mixed: bfloat16 [8192, 6144], P('ctx', 'dp')
The draws below stay inside these ranges and needn't reach their ends.
Inputs may be any that keep to these rules, and one draw needn't show every extreme that they name: `key_tiles`: tiles have coordinates (frame layer, height, width) on a grid of 16 x 2 x 4, tile number (layer * 2 + height) * 4 + width. For each head and query tile, the first key_counts entries are distinct tiles that differ from the query tile by at most one in each coordinate, the query tile itself among them; the other entries repeat the query tile. In every head some tile lists its whole window.
All inputs are finite; a program needn't handle non-finite values.
Results may differ from the reference program's by a relative error of at most 0.0088.
Values may be sent and summed in bfloat16 or wider, within the bound.
A program may use at most 64 MiB of HBM per device.

```python
import math
import jax
import jax.numpy as jnp
from jax import lax

D = 6144
HEAD_DIM = 128
HEADS = 32
TILE = 64
TH = 2
TW = 4
MAXK = 18
TILES = 128
CLIP_LEN = 8192


def window_lists(key):
    base = jax.random.fold_in(key, 11)
    layers = TILES // (TH * TW)
    grid = jnp.arange(TILES, dtype=jnp.int32)
    layer = grid // (TH * TW)
    row_pos = grid // TW % TH
    col_pos = grid % TW
    shifts = jnp.arange(27, dtype=jnp.int32)
    step_t = shifts // 9 - 1
    step_h = shifts // 3 % 3 - 1
    step_w = shifts % 3 - 1
    near_t = layer[:, None] + step_t[None, :]
    near_h = row_pos[:, None] + step_h[None, :]
    near_w = col_pos[:, None] + step_w[None, :]
    inside = (near_t >= 0) & (near_t < layers) & (near_h >= 0) & (near_h < TH) & (near_w >= 0) & (near_w < TW)
    near_id = (near_t * TH + near_h) * TW + near_w
    itself = shifts == 13
    forced = (layer == 1) & (row_pos == min(1, TH - 1)) & (col_pos == min(1, TW - 1))
    coins = jax.random.randint(base, (HEADS, TILES, 27), 0, 4)
    kept = inside[None] & ((coins != 0) | itself[None, None, :] | forced[None, :, None])
    counts = jnp.sum(kept.astype(jnp.int32), axis=-1)
    ranks = jnp.where(kept, shifts, shifts + 27)
    order = jnp.argsort(ranks, axis=-1, stable=True)[..., :MAXK]
    chosen = jnp.take_along_axis(jnp.broadcast_to(near_id, kept.shape), order, axis=-1)
    slots = jnp.arange(MAXK, dtype=jnp.int32)
    listed = jnp.where(slots[None, None, :] < counts[..., None], chosen, grid[None, :, None])
    return (listed.astype(jnp.int32), counts.astype(jnp.int32))


def draw_key_tiles(key, part):
    return window_lists(key)[0]


def draw_key_counts(key, part):
    return window_lists(key)[1]


def levels(rng, shape, shards, smallest, high):
    factor_of, own = 1.0, jax.random.fold_in(rng, 6)
    for axis_at, parts in shards:
        heights = jnp.exp(jax.random.uniform(jax.random.fold_in(own, axis_at), (parts,), jnp.float32, smallest / len(shards), high / len(shards)))
        factor_of = factor_of * jnp.repeat(heights, shape[axis_at] // parts).reshape([-1 if axis == axis_at else 1 for axis in range(len(shape))])
    return factor_of


def bell_draw(key, extent, scale, most, split=(), kind=jnp.bfloat16):
    values = jax.random.normal(key, extent, jnp.float32) * scale
    if len(split) > 0:
        values = levels(key, extent, split, -0.22, 0.18) * values
    return jnp.clip(values, min=-most, max=most).astype(kind)


def setup_inputs(seed: int = 0) -> dict:
    streams_of = jax.random.split(jax.random.key(seed), 8)
    return {
        "frames": bell_draw(streams_of[0], (CLIP_LEN, D), 1.0, 6.0, ((0, 16),)),
        "proj_weight": bell_draw(streams_of[1], (3, D, HEADS * HEAD_DIM), D ** -0.5, 0.078125, ((1, 16), (2, 16))),
        "out_weight": bell_draw(streams_of[2], (D, HEADS * HEAD_DIM), (HEADS * HEAD_DIM) ** -0.5, 0.09375, ((0, 16), (1, 16))),
        "query_gain": jnp.clip(jnp.exp(math.log(2.0) - 1.3862944 * jax.random.uniform(streams_of[3], (HEADS * HEAD_DIM,), jnp.float32) ** levels(streams_of[3], (HEADS * HEAD_DIM,), ((0, 16),), -0.2, 0.2)), 0.5, 2.0),
        "key_gain": jnp.clip(jnp.exp(math.log(2.0) - 1.3862944 * jax.random.uniform(streams_of[4], (HEADS * HEAD_DIM,), jnp.float32) ** levels(streams_of[4], (HEADS * HEAD_DIM,), ((0, 16),), -0.2, 0.2)), 0.5, 2.0),
        "key_tiles": draw_key_tiles(jax.random.fold_in(streams_of[7], 71), 0),
        "key_counts": draw_key_counts(jax.random.fold_in(streams_of[7], 71), 0),
    }


eps = 1e-06

def normed(rows, gain):
    stat = lax.optimization_barrier(jnp.mean(rows * rows, axis=-1, keepdims=True))
    return rows * lax.rsqrt(stat + eps) * gain

def attend_head(inputs):
    query_rows, key_rows, value_rows, tile_ids, tile_counts = inputs
    query_tiles = query_rows.reshape(-1, TILE, HEAD_DIM).astype(jnp.float32)
    key_tiles = key_rows.reshape(-1, TILE, HEAD_DIM)
    value_tiles = value_rows.reshape(-1, TILE, HEAD_DIM)
    local_ids = tile_ids.astype(jnp.int32)
    count_q = query_tiles.shape[0]
    picked_keys = key_tiles[local_ids].reshape(count_q, MAXK * TILE, HEAD_DIM).astype(jnp.float32)
    picked_values = value_tiles[local_ids].reshape(count_q, MAXK * TILE, HEAD_DIM).astype(jnp.float32)
    scores = jnp.einsum('qtd,qsd->qts', query_tiles, picked_keys) * HEAD_DIM ** (-0.5)
    live = (jnp.arange(MAXK, dtype=jnp.int32)[None, :] < tile_counts[:, None]).astype(jnp.float32)
    live = jnp.repeat(live, TILE, axis=1)[:, None, :]
    weights = jnp.exp(scores) * live
    totals = lax.optimization_barrier(jnp.sum(weights, axis=-1, keepdims=True))
    rounded = lax.optimization_barrier(weights.astype(jnp.bfloat16)).astype(jnp.float32)
    summed = jnp.einsum('qts,qsd->qtd', rounded, picked_values) / totals
    return summed.astype(jnp.bfloat16).reshape(-1, HEAD_DIM)

def reference(frames, proj_weight, out_weight, query_gain, key_gain, key_tiles, key_counts):
    width = HEADS * HEAD_DIM
    query_full = jnp.dot(frames, proj_weight[0], preferred_element_type=jnp.float32)
    query_rows = normed(query_full.reshape(-1, HEADS, HEAD_DIM), query_gain.reshape(HEADS, HEAD_DIM)).astype(jnp.bfloat16)
    key_full = jnp.dot(frames, proj_weight[1], preferred_element_type=jnp.float32)
    key_rows = normed(key_full.reshape(-1, HEADS, HEAD_DIM), key_gain.reshape(HEADS, HEAD_DIM)).astype(jnp.bfloat16)
    value_rows = jnp.dot(frames, proj_weight[2], preferred_element_type=jnp.float32).astype(jnp.bfloat16).reshape(-1, HEADS, HEAD_DIM)
    attended = lax.map(attend_head, (query_rows.transpose(1, 0, 2), key_rows.transpose(1, 0, 2), value_rows.transpose(1, 0, 2), key_tiles, key_counts))
    attended = attended.transpose(1, 0, 2).reshape(-1, width)
    result = lax.dot_general(attended, out_weight, (((1,), (1,)), ((), ())), preferred_element_type=jnp.float32)
    return result.astype(jnp.bfloat16)
```

```python
import math

import jax
import jax.numpy as jnp
from jax import lax
from jax.experimental import pallas as pl
from jax.experimental.pallas import tpu as pltpu
from jax.sharding import PartitionSpec as P

MESH = pl.DeviceIdType.MESH
F32, BF16 = jnp.float32, jnp.bfloat16

D = 6144
HD = 128
TILE = 64
TOK = 512
QT = 8
SLOTS = 18
NZ = 8
NX = 4
NY = 4
NC = 16
ROWS = 384
HALF = 192
KEYS = 3 * TOK
EPS = 1e-06
SCALE = math.log2(math.e) / math.sqrt(HD)

ROUNDS = ((1, 0), (2, 0), (0, 0), (1, 1), (2, 1), (0, 1), (3, 0), (3, 1))


def kernel(fr_hbm, pw_hbm, ow_hbm, qg, kg, kt, kc, out, wg, fr, acc, qbuf, kv, att, mask, oacc,
           fsem, osem, zsend, zrecv, bsend, brecv, hsend, hrecv, gsend, grecv):
    dp, c = lax.axis_index("dp"), lax.axis_index("ctx")
    z, core = c // 2, c % 2
    x, y = dp % NX, dp // NX
    sib = (dp, z * 2 + 1 - core)
    prv, nxt = (dp, (c + NC - 1) % NC), (dp, (c + 1) % NC)

    def zdev(step):
        return (dp, ((z + step + NZ) % NZ) * 2 + core)

    def xydev(i, j):
        return (((y + j + NY) % NY) * NX + (x + i + NX) % NX, c)

    frames = pltpu.make_async_copy(fr_hbm, fr, fsem)
    own = []
    for r, (j, h) in enumerate(ROUNDS):
        cols = pl.ds(h * HD, HD)
        src = ow_hbm.at[:, cols] if j == 3 else pw_hbm.at[j, :, cols]
        own.append(pltpu.make_async_copy(src, wg.at[r, c], osem.at[r]))
    for copy in own:
        copy.start()
    frames.start()

    barrier = pltpu.get_barrier_semaphore()
    greeted = [zdev(1), zdev(-1), prv, nxt, xydev(1, 0), xydev(-1, 0), xydev(0, 1), xydev(0, -1)]
    for device in greeted:
        pl.semaphore_signal(barrier, inc=1, device_id=device, device_id_type=MESH)
    pl.semaphore_wait(barrier, len(greeted))

    def zcopy(direction, r, owner, hop, half=False):
        piece = wg.at[r, owner * 2 + core]
        if half:
            piece = piece.at[pl.ds(direction * HALF, HALF)]
        return pltpu.make_async_remote_copy(
            src_ref=piece, dst_ref=piece, send_sem=zsend, recv_sem=zrecv.at[direction, r, hop],
            device_id=zdev(1 - 2 * direction), device_id_type=MESH,
        )

    def bcopy(r, owner, which):
        piece = wg.at[r, owner * 2 + which]
        return pltpu.make_async_remote_copy(
            src_ref=piece, dst_ref=piece, send_sem=bsend, recv_sem=brecv.at[r, owner],
            device_id=sib, device_id_type=MESH,
        )

    def send_own(r):
        zcopy(0, r, z, 0).start()
        zcopy(1, r, z, 0).start()
        bcopy(r, z, core).start()

    def zat(step):
        return (z + step + NZ) % NZ

    for copy in own:
        copy.wait()
    send_own(0)
    send_own(1)

    lane_tile = lax.broadcasted_iota(jnp.int32, (QT, KEYS), 1) // TILE + (c - 1) * QT
    row = lax.broadcasted_iota(jnp.int32, (QT, QT), 0)
    col = lax.broadcasted_iota(jnp.int32, (QT, QT), 1)
    for h in range(2):
        counts = jnp.sum(
            jnp.where(row == col, kc[h:h + 1, :].astype(F32), 0.0), axis=1, keepdims=True
        ).astype(jnp.int32)
        listed = jnp.zeros((QT, KEYS), F32)
        for s in range(SLOTS):
            tile = jnp.where(s < counts, kt[h, :, s:s + 1], -1000)
            listed = jnp.where(lane_tile == tile, 1.0, listed)
        for i in range(QT):
            mask[h, i] = listed[i:i + 1, :]

    frames.wait()

    def project(r, owner, first=False):
        cols = pl.ds(pl.multiple_of(owner * (2 * ROWS), 2 * ROWS), 2 * ROWS)
        weight = wg[r, pl.ds(owner * 2, 2)].reshape(2 * ROWS, HD)
        part = jnp.dot(fr[:, cols], weight, preferred_element_type=F32)
        if first:
            acc[r] = part
        else:
            acc[r] += part

    def normed(r, gain):
        rows = acc[r]
        stat = jnp.mean(rows * rows, axis=-1, keepdims=True)
        return (rows * lax.rsqrt(stat + EPS) * gain).astype(BF16)

    def halo(h, which, side):
        slot = 2 - 2 * side
        return pltpu.make_async_remote_copy(
            src_ref=kv.at[h, which, 1], dst_ref=kv.at[h, which, slot], send_sem=hsend,
            recv_sem=hrecv.at[h, which, side], device_id=(prv, nxt)[side], device_id_type=MESH,
        )

    def send_halo(h, which):
        halo(h, which, 0).start()
        halo(h, which, 1).start()

    def attention(h):
        for which in range(2):
            for side in range(2):
                halo(h, which, side).wait_recv()

        def block(b, carry):
            rows = pl.ds(pl.multiple_of(b * 128, 128), 128)
            keys = kv[h, 0].reshape(KEYS, HD)
            values = kv[h, 1].reshape(KEYS, HD)
            scores = lax.dot_general(
                qbuf[rows, :], keys, (((1,), (1,)), ((), ())), preferred_element_type=F32
            )
            live = jnp.concatenate(
                [jnp.broadcast_to(mask[h, b * 2 + i], (TILE, KEYS)) for i in range(2)], axis=0
            )
            weights = jnp.where(live > 0.5, jnp.exp2(scores * SCALE), 0.0)
            total = jnp.sum(weights, axis=-1, keepdims=True)
            summed = jnp.dot(weights.astype(BF16), values, preferred_element_type=F32)
            att[h, dp, rows, :] = (summed / total).astype(BF16)
            return carry

        lax.fori_loop(0, TOK // 128, block, 0)

    def gcopy(h, part, stage, direction, hop, across, along):
        i, j = (across, along) if part == 0 else (along, across)
        owner = ((y + j + NY) % NY) * NX + (x + i + NX) % NX
        start, size = part * 256, 256
        if hop == 1:
            start, size = start + direction * 128, 128
        piece = att.at[h, owner, pl.ds(start, size)]
        step = 1 - 2 * direction
        on_first = stage == 0
        target = xydev(step, 0) if on_first == (part == 0) else xydev(0, step)
        return pltpu.make_async_remote_copy(
            src_ref=piece, dst_ref=piece, send_sem=gsend,
            recv_sem=grecv.at[h, part, stage, direction, hop], device_id=target, device_id_type=MESH,
        )

    OFF = (0, -1, 1, 2)

    def first_send(h, part, direction, hop):
        gcopy(h, part, 0, direction, hop, 0 if hop == 0 else (-1 if direction == 0 else 1), 0).start()

    def first_wait(h, part, direction, hop):
        away = 2 if hop == 1 else (-1 if direction == 0 else 1)
        gcopy(h, part, 0, direction, hop, away, 0).wait_recv()

    def second_send(h, part, k, direction, hop):
        along = 0 if hop == 0 else (-1 if direction == 0 else 1)
        gcopy(h, part, 1 + k, direction, hop, OFF[k], along).start()

    def second_wait(h, part, k, direction, hop):
        along = 2 if hop == 1 else (-1 if direction == 0 else 1)
        gcopy(h, part, 1 + k, direction, hop, OFF[k], along).wait_recv()

    both = [(part, direction) for part in range(2) for direction in range(2)]

    def gather0(h):
        for part, direction in both:
            first_send(h, part, direction, 0)
        for part, direction in both:
            second_send(h, part, 0, direction, 0)

    def gather1(h):
        for part, direction in both:
            first_wait(h, part, direction, 0)
            first_send(h, part, direction, 1)
            for d in range(2):
                second_send(h, part, 1 + direction, d, 0)
        for part, direction in both:
            second_wait(h, part, 0, direction, 0)
            second_send(h, part, 0, direction, 1)

    def gather2(h):
        for part in range(2):
            for direction in range(2):
                first_wait(h, part, direction, 1)
            for d in range(2):
                second_send(h, part, 3, d, 0)
        for k in (1, 2):
            for part, direction in both:
                second_wait(h, part, k, direction, 0)
                second_send(h, part, k, direction, 1)

    def gather3(h):
        for part, direction in both:
            second_wait(h, part, 3, direction, 0)
            second_send(h, part, 3, direction, 1)
        for k in (0, 1, 2):
            for part, direction in both:
                second_wait(h, part, k, direction, 1)

    def gather4(h):
        for part, direction in both:
            second_wait(h, part, 3, direction, 1)

    def tick(t, carry):
        p, s = t // 4, t % 4 + 1
        for lane in range(2):
            r = 2 * p + lane

            @pl.when(s < 4)
            def _():
                zcopy(0, r, zat(-s), s - 1).wait_recv()

                @pl.when(s < 3)
                def _():
                    zcopy(0, r, zat(-s), s).start()

                @pl.when(s == 3)
                def _():
                    zcopy(0, r, zat(-s), 3, True).start()

                bcopy(r, zat(-s), core).start()
                zcopy(1, r, zat(s), s - 1).wait_recv()

                @pl.when(s < 3)
                def _():
                    zcopy(1, r, zat(s), s).start()

                @pl.when(s == 3)
                def _():
                    zcopy(1, r, zat(s), 3, True).start()

                bcopy(r, zat(s), core).start()

            @pl.when(s == 4)
            def _():
                @pl.when(p < 3)
                def _():
                    send_own(r + 2)

                zcopy(0, r, zat(4), 3, True).wait_recv()
                zcopy(1, r, zat(4), 3, True).wait_recv()
                bcopy(r, zat(4), core).start()

        for step, gather in ((1, gather1), (2, gather2), (3, gather3), (4, gather4)):
            @pl.when((p >= 2) & (s == step))
            def _():
                gather(p - 2)

        for lane in range(2):
            r = 2 * p + lane

            @pl.when(s == 1)
            def _():
                bcopy(r, z, 1 - core).wait_recv()

                @pl.when(p < 3)
                def _():
                    project(r, z, first=True)

            bcopy(r, zat(-s), 1 - core).wait_recv()

            @pl.when(s < 4)
            def _():
                bcopy(r, zat(s), 1 - core).wait_recv()

            @pl.when(p < 3)
            def _():
                project(r, zat(-s))

                @pl.when(s < 4)
                def _():
                    project(r, zat(s))

        @pl.when((s == 4) & (p == 0))
        def _():
            kv[0, 0, 1] = normed(0, kg[0:1, :])
            send_halo(0, 0)
            kv[0, 1, 1] = acc[1].astype(BF16)
            send_halo(0, 1)

        @pl.when((s == 4) & (p == 1))
        def _():
            kv[1, 0, 1] = normed(3, kg[1:2, :])
            send_halo(1, 0)
            qbuf[...] = normed(2, qg[0:1, :])

        @pl.when((s == 4) & (p == 2))
        def _():
            kv[1, 1, 1] = acc[4].astype(BF16)
            send_halo(1, 1)
            qbuf[...] = normed(5, qg[1:2, :])

        @pl.when((s == 4) & (p >= 1) & (p < 3))
        def _():
            attention(p - 1)
            gather0(p - 1)

        return carry

    lax.fori_loop(0, 16, tick, 0)

    oacc[...] = jnp.zeros_like(oacc)

    def mix(i, carry):
        h, d = i // 4, i % 4 * 4
        left = jnp.concatenate([att[h, d + k] for k in range(4)], axis=1)
        right = jnp.concatenate([wg[6 + h, d + k] for k in range(4)], axis=1)
        oacc[...] += lax.dot_general(
            left, right, (((1,), (1,)), ((), ())), preferred_element_type=F32
        )
        return carry

    lax.fori_loop(0, 8, mix, 0)
    out[...] = oacc[...].astype(BF16)

    for sent, sem in (
        (wg.at[pl.ds(0, 7), pl.ds(0, 8)], zsend),
        (wg.at[pl.ds(0, 4)], bsend),
        (kv.at[:, :, pl.ds(0, 2)], hsend),
        (att.at[:, pl.ds(0, 15)], gsend),
    ):
        pltpu.make_async_copy(sent, sent, sem).wait()


def body(frames, proj_weight, out_weight, query_gain, key_gain, key_tiles, key_counts):
    anywhere = pl.BlockSpec(memory_space=pl.ANY)
    vmem = pl.BlockSpec(memory_space=pltpu.VMEM)
    dma = pltpu.SemaphoreType.DMA
    return pl.pallas_call(
        kernel,
        out_shape=jax.ShapeDtypeStruct((TOK, ROWS), BF16),
        in_specs=[anywhere] * 3 + [vmem] * 4,
        out_specs=vmem,
        scratch_shapes=[
            pltpu.VMEM((8, NC, ROWS, HD), BF16),
            pltpu.VMEM((TOK, D), BF16),
            pltpu.VMEM((6, TOK, HD), F32),
            pltpu.VMEM((TOK, HD), BF16),
            pltpu.VMEM((2, 2, 3, TOK, HD), BF16),
            pltpu.VMEM((2, 16, TOK, HD), BF16),
            pltpu.VMEM((2, QT, 1, KEYS), F32),
            pltpu.VMEM((TOK, ROWS), F32),
            dma, dma((8,)),
            dma, dma((2, 8, 4)),
            dma, dma((8, 8)),
            dma, dma((2, 2, 2)),
            dma, dma((2, 2, 5, 2, 2)),
        ],
        compiler_params=pltpu.CompilerParams(
            collective_id=0, has_side_effects=True, vmem_limit_bytes=56 * 2**20
        ),
        cost_estimate=pl.CostEstimate(
            flops=8 * 10**9, bytes_accessed=8 * 10**6, transcendentals=2 * 10**6
        ),
        name="layer",
    )(
        frames, proj_weight, out_weight, query_gain.reshape(2, HD), key_gain.reshape(2, HD),
        key_tiles, key_counts,
    )


def solution(mesh):
    placed = (
        P("ctx", None),
        P(None, "ctx", "dp"),
        P("dp", "ctx"),
        P("dp"),
        P("dp"),
        P("dp", "ctx", None),
        P("dp", "ctx"),
    )
    return jax.shard_map(
        body, mesh=mesh, in_specs=placed, out_specs=P("ctx", "dp"), check_vma=False
    )
```

```python
import math

import jax
import jax.numpy as jnp
from jax import lax
from jax.experimental import pallas as pl
from jax.experimental.pallas import tpu as pltpu
from jax.sharding import PartitionSpec as P

MESH = pl.DeviceIdType.MESH
F32, BF16 = jnp.float32, jnp.bfloat16

D = 6144
HD = 128
TILE = 64
TOK = 512
QT = 8
SLOTS = 18
NZ = 8
NX = 4
NY = 4
NC = 16
ROWS = 384
HALF = 192
KEYS = 3 * TOK
EPS = 1e-06
SCALE = math.log2(math.e) / math.sqrt(HD)

ROUNDS = ((1, 0), (2, 0), (0, 0), (1, 1), (2, 1), (0, 1), (3, 0), (3, 1))


def kernel(fr_hbm, pw_hbm, ow_hbm, qg, kg, kt, kc, out, wg, fr, acc, qbuf, kv, att, mask, oacc, part_sum, part_lanes,
           fsem, osem, zsend, zrecv, bsend, brecv, hsend, hrecv, gsend, grecv):
    dp, c = lax.axis_index("dp"), lax.axis_index("ctx")
    z, core = c // 2, c % 2
    x, y = dp % NX, dp // NX
    sib = (dp, z * 2 + 1 - core)
    prv, nxt = (dp, (c + NC - 1) % NC), (dp, (c + 1) % NC)

    def zdev(step):
        return (dp, ((z + step + NZ) % NZ) * 2 + core)

    def xydev(i, j):
        return (((y + j + NY) % NY) * NX + (x + i + NX) % NX, c)

    frames = pltpu.make_async_copy(fr_hbm, fr, fsem)
    own = []
    for r, (j, h) in enumerate(ROUNDS):
        cols = pl.ds(h * HD, HD)
        src = ow_hbm.at[:, cols] if j == 3 else pw_hbm.at[j, :, cols]
        own.append(pltpu.make_async_copy(src, wg.at[r, c], osem.at[r]))
    for copy in own:
        copy.start()
    frames.start()

    barrier = pltpu.get_barrier_semaphore()
    greeted = [zdev(1), zdev(-1), prv, nxt]
    greeted += [xydev(i, 0) for i in (-1, 1, 2)] + [xydev(0, j) for j in (-1, 1, 2)]
    for device in greeted:
        pl.semaphore_signal(barrier, inc=1, device_id=device, device_id_type=MESH)
    pl.semaphore_wait(barrier, len(greeted))

    def zcopy(direction, r, owner, hop, half=False):
        piece = wg.at[r, owner * 2 + core]
        if half:
            piece = piece.at[pl.ds(direction * HALF, HALF)]
        return pltpu.make_async_remote_copy(
            src_ref=piece, dst_ref=piece, send_sem=zsend, recv_sem=zrecv.at[direction, r, hop],
            device_id=zdev(1 - 2 * direction), device_id_type=MESH,
        )

    def bcopy(r, owner, which):
        piece = wg.at[r, owner * 2 + which]
        return pltpu.make_async_remote_copy(
            src_ref=piece, dst_ref=piece, send_sem=bsend, recv_sem=brecv.at[r, owner],
            device_id=sib, device_id_type=MESH,
        )

    def send_own(r):
        zcopy(0, r, z, 0).start()
        zcopy(1, r, z, 0).start()
        bcopy(r, z, core).start()

    def zat(step):
        return (z + step + NZ) % NZ

    for copy in own:
        copy.wait()
    for r in range(3):
        send_own(r)

    lane_tile = lax.broadcasted_iota(jnp.int32, (QT, KEYS), 1) // TILE + (c - 1) * QT
    row = lax.broadcasted_iota(jnp.int32, (QT, QT), 0)
    col = lax.broadcasted_iota(jnp.int32, (QT, QT), 1)
    for h in range(2):
        counts = jnp.sum(
            jnp.where(row == col, kc[h:h + 1, :].astype(F32), 0.0), axis=1, keepdims=True
        ).astype(jnp.int32)
        listed = jnp.zeros((QT, KEYS), F32)
        for s in range(SLOTS):
            tile = jnp.where(s < counts, kt[h, :, s:s + 1], -1000)
            listed = jnp.where(lane_tile == tile, 1.0, listed)
        for i in range(QT):
            for slot in range(3):
                mask[h, slot, i] = listed[i:i + 1, slot * TOK:(slot + 1) * TOK]

    def project(r, owner, first=False):
        cols = pl.ds(pl.multiple_of(owner * (2 * ROWS), 2 * ROWS), 2 * ROWS)
        weight = wg[r, pl.ds(owner * 2, 2)].reshape(2 * ROWS, HD)
        part = jnp.dot(fr[:, cols], weight, preferred_element_type=F32)
        if first:
            acc[r] = part
        else:
            acc[r] += part

    def normed(r, gain):
        rows = acc[r]
        stat = jnp.mean(rows * rows, axis=-1, keepdims=True)
        return (rows * lax.rsqrt(stat + EPS) * gain).astype(BF16)

    def halo(h, which, side):
        return pltpu.make_async_remote_copy(
            src_ref=kv.at[h, which, 1], dst_ref=kv.at[h, which, 2 - 2 * side], send_sem=hsend,
            recv_sem=hrecv.at[h, which, side], device_id=(dp, (c + NC - 1 + 2 * side) % NC),
            device_id_type=MESH,
        )

    def send_halo(h, which):
        halo(h, which, 1 - core).start()
        halo(h, which, core).start()

    def weigh(h, b, slot):
        rows = pl.ds(pl.multiple_of(b * 128, 128), 128)
        scores = lax.dot_general(
            qbuf[rows, :], kv[h, 0, slot], (((1,), (1,)), ((), ())), preferred_element_type=F32
        )
        live = jnp.concatenate(
            [jnp.broadcast_to(mask[h, slot, b * 2 + i], (TILE, TOK)) for i in range(2)], axis=0
        )
        weights = jnp.where(live > 0.5, jnp.exp2(scores * SCALE), 0.0)
        lanes = sum(weights[:, i * HD:(i + 1) * HD] for i in range(TOK // HD))
        summed = jnp.dot(weights.astype(BF16), kv[h, 1, slot], preferred_element_type=F32)
        return summed, lanes

    def attend_near(h):
        for which in range(2):
            halo(h, which, core).wait_recv()

        def near(b, carry):
            rows = pl.ds(pl.multiple_of(b * 128, 128), 128)
            summed, lanes = weigh(h, b, 1)
            more, more_lanes = weigh(h, b, 2 - 2 * core)
            part_sum[rows, :] = summed + more
            part_lanes[rows, :] = lanes + more_lanes
            return carry

        lax.fori_loop(0, TOK // 128, near, 0)

    def attend_far(h, part):
        if part == 0:
            for which in range(2):
                halo(h, which, 1 - core).wait_recv()

        def far(b, carry):
            rows = pl.ds(pl.multiple_of(b * 128, 128), 128)
            summed, lanes = weigh(h, b, 2 * core)
            total = jnp.sum(part_lanes[rows, :] + lanes, axis=-1, keepdims=True)
            att[h, dp, rows, :] = ((part_sum[rows, :] + summed) / total).astype(BF16)
            return carry

        lax.fori_loop(2 * part, 2 * part + 2, far, 0)
        gather0(h, part)

    def gcopy(h, part, stage, direction, hop, across, along, half, step):
        i, j = (across, along) if part == 0 else (along, across)
        owner = ((y + j + NY) % NY) * NX + (x + i + NX) % NX
        start, size = part * 256, 256
        if half:
            start, size = start + direction * 128, 128
        piece = att.at[h, owner, pl.ds(start, size)]
        target = xydev(step, 0) if (stage == 0) == (part == 0) else xydev(0, step)
        return pltpu.make_async_remote_copy(
            src_ref=piece, dst_ref=piece, send_sem=gsend,
            recv_sem=grecv.at[h, part, stage, direction, hop], device_id=target, device_id_type=MESH,
        )

    OFF = (0, -1, 1, 2)
    PASSED = ((), (0, 1, 2))

    def first_send(h, part):
        for direction in range(2):
            gcopy(h, part, 0, direction, 0, 0, 0, False, 1 - 2 * direction).start()
        gcopy(h, part, 0, 0, 1, 0, 0, False, 2).start()

    def first_wait(h, part, k):
        gcopy(h, part, 0, (0, 0, 1, 0)[k], k // 3, OFF[k], 0, False, 1).wait_recv()

    def second_send(h, part, k):
        for direction in range(2):
            gcopy(h, part, 1 + k, direction, 0, OFF[k], 0, False, 1 - 2 * direction).start()
        if k not in PASSED[h]:
            gcopy(h, part, 1 + k, 0, 1, OFF[k], 0, False, 2).start()

    def second_pass(h, part, k):
        for direction in range(2):
            step = 1 - 2 * direction
            gcopy(h, part, 1 + k, direction, 0, OFF[k], -step, False, step).wait_recv()
            gcopy(h, part, 1 + k, direction, 1, OFF[k], -step, True, step).start()

    def second_wait(h, part, k):
        if k in PASSED[h]:
            for direction in range(2):
                gcopy(h, part, 1 + k, direction, 1, OFF[k], 2, True, 1).wait_recv()
        else:
            for direction in range(2):
                step = 1 - 2 * direction
                gcopy(h, part, 1 + k, direction, 0, OFF[k], -step, False, step).wait_recv()
            gcopy(h, part, 1 + k, 0, 1, OFF[k], 2, False, 1).wait_recv()

    def gather0(h, part):
        first_send(h, part)
        second_send(h, part, 0)

    def gather1(h):
        for k in (1, 2, 3):
            for part in range(2):
                first_wait(h, part, k)
                second_send(h, part, k)
        if 0 in PASSED[h]:
            for part in range(2):
                second_pass(h, part, 0)

    def gather2(h):
        for k in PASSED[h]:
            if k > 0:
                for part in range(2):
                    second_pass(h, part, k)

    def pass_on(r, s):
        if s == 4:
            zcopy(0, r, zat(4), 3, True).wait_recv()
            zcopy(1, r, zat(4), 3, True).wait_recv()
            bcopy(r, zat(4), core).start()
            return
        for direction in range(2):
            owner = zat(-s if direction == 0 else s)
            zcopy(direction, r, owner, s - 1).wait_recv()
            zcopy(direction, r, owner, s, s == 3).start()
            bcopy(r, owner, core).start()

    def from_sibling(r, owner):
        bcopy(r, owner, 1 - core).wait_recv()

    def add(r, s, rounds=1):
        owners = {0: 1, 4: 1}.get(s, 2)

        def step(i, carry):
            at = r + i // owners
            owner = zat(s * (2 * (i % owners) - 1))
            from_sibling(at, owner)
            project(at, owner, first=s == 0)
            return carry

        lax.fori_loop(0, rounds * owners, step, 0)

    def finish_keys(g):
        add(3 * g, 4)
        kv[g, 0, 1] = normed(3 * g, kg[g:g + 1, :])
        send_halo(g, 0)
        add(3 * g + 1, 4)
        kv[g, 1, 1] = acc[3 * g + 1].astype(BF16)
        send_halo(g, 1)

    def finish_query(g):
        add(3 * g + 2, 4)
        qbuf[...] = normed(3 * g + 2, qg[g:g + 1, :])

    def mix(h, part, k):
        rows = pl.ds(part * 256, 256)
        owners = []
        for j in range(4):
            if part == 0:
                owners.append(j * NX + (x + OFF[k] + NX) % NX)
            else:
                owners.append((y + OFF[k] + NY) % NY * NX + j)
        left = jnp.concatenate([att[h, owner, rows, :] for owner in owners], axis=1)
        right = jnp.concatenate([wg[6 + h, owner] for owner in owners], axis=1)
        mixed = lax.dot_general(
            left, right, (((1,), (1,)), ((), ())), preferred_element_type=F32
        )
        if h == 0 and k == 0:
            oacc[rows, :] = mixed
        elif h == 1 and k == 3:
            out[rows, :] = (oacc[rows, :] + mixed).astype(BF16)
        else:
            oacc[rows, :] += mixed

    frames.wait()
    add(0, 0, 3)
    for g in range(2):
        k, v, q, before = 3 * g, 3 * g + 1, 3 * g + 2, 3 * g - 1
        pass_on(k, 1)
        pass_on(v, 1)
        if g == 1:
            send_own(q)
            pass_on(before, 4)
            add(k, 0, 3)
        add(k, 1, 2)
        if g == 1:
            finish_query(0)
            attend_near(0)
        pass_on(k, 2)
        pass_on(v, 2)
        if g == 1:
            attend_far(0, 0)
        pass_on(q, 1)
        if g == 1:
            attend_far(0, 1)
        add(k, 2, 2)
        add(q, 1)
        pass_on(k, 3)
        pass_on(v, 3)
        pass_on(q, 2)
        if g == 0:
            send_own(3)
            send_own(4)
        add(k, 3, 2)
        add(q, 2)
        if g == 1:
            gather1(0)
        pass_on(q, 3)
        pass_on(k, 4)
        pass_on(v, 4)
        finish_keys(g)
        if g == 1:
            send_own(6)
            send_own(7)
        add(q, 3)
    pass_on(5, 4)
    finish_query(1)
    attend_near(1)
    attend_far(1, 0)
    attend_far(1, 1)
    for s in range(1, 5):
        for r in (6, 7):
            pass_on(r, s)
        if s == 2:
            gather1(1)
        if s == 3:
            gather2(1)
    for r in (6, 7):
        for owner in range(NZ):
            from_sibling(r, owner)
    gather2(0)
    for h in range(2):
        for k in range(4):
            for part in range(2):
                second_wait(h, part, k)
                mix(h, part, k)

    for sent, sem in (
        (wg.at[pl.ds(0, 7), pl.ds(0, 8)], zsend),
        (wg.at[pl.ds(0, 4)], bsend),
        (kv.at[:, :, pl.ds(0, 2)], hsend),
        (att.at[:, pl.ds(0, 15)], gsend),
    ):
        pltpu.make_async_copy(sent, sent, sem).wait()


def body(frames, proj_weight, out_weight, query_gain, key_gain, key_tiles, key_counts):
    anywhere = pl.BlockSpec(memory_space=pl.ANY)
    vmem = pl.BlockSpec(memory_space=pltpu.VMEM)
    dma = pltpu.SemaphoreType.DMA
    return pl.pallas_call(
        kernel,
        out_shape=jax.ShapeDtypeStruct((TOK, ROWS), BF16),
        in_specs=[anywhere] * 3 + [vmem] * 4,
        out_specs=vmem,
        scratch_shapes=[
            pltpu.VMEM((8, NC, ROWS, HD), BF16),
            pltpu.VMEM((TOK, D), BF16),
            pltpu.VMEM((6, TOK, HD), F32),
            pltpu.VMEM((TOK, HD), BF16),
            pltpu.VMEM((2, 2, 3, TOK, HD), BF16),
            pltpu.VMEM((2, 16, TOK, HD), BF16),
            pltpu.VMEM((2, 3, QT, 1, TOK), F32),
            pltpu.VMEM((TOK, ROWS), F32),
            pltpu.VMEM((TOK, HD), F32),
            pltpu.VMEM((TOK, HD), F32),
            dma, dma((8,)),
            dma, dma((2, 8, 4)),
            dma, dma((8, 8)),
            dma, dma((2, 2, 2)),
            dma, dma((2, 2, 5, 2, 2)),
        ],
        compiler_params=pltpu.CompilerParams(
            collective_id=0, has_side_effects=True, vmem_limit_bytes=56 * 2**20
        ),
        cost_estimate=pl.CostEstimate(
            flops=8 * 10**9, bytes_accessed=8 * 10**6, transcendentals=2 * 10**6
        ),
        name="layer",
    )(
        frames, proj_weight, out_weight, query_gain.reshape(2, HD), key_gain.reshape(2, HD),
        key_tiles, key_counts,
    )


def solution(mesh):
    placed = (
        P("ctx", None),
        P(None, "ctx", "dp"),
        P("dp", "ctx"),
        P("dp"),
        P("dp"),
        P("dp", "ctx", None),
        P("dp", "ctx"),
    )
    return jax.shard_map(
        body, mesh=mesh, in_specs=placed, out_specs=P("ctx", "dp"), check_vma=False
    )
```

```python
import math

import jax
import jax.numpy as jnp
from jax import lax
from jax.experimental import pallas as pl
from jax.experimental.pallas import tpu as pltpu
from jax.sharding import PartitionSpec as P

MESH = pl.DeviceIdType.MESH
F32, BF16 = jnp.float32, jnp.bfloat16

D = 6144
HD = 128
TILE = 64
TOK = 512
QT = 8
SLOTS = 18
NZ = 8
NX = 4
NY = 4
NC = 16
ROWS = 384
HALF = 192
KEYS = 3 * TOK
EPS = 1e-06
SCALE = math.log2(math.e) / math.sqrt(HD)

ROUNDS = ((1, 0), (2, 0), (0, 0), (1, 1), (2, 1), (0, 1), (3, 0), (3, 1))


def kernel(fr_hbm, pw_hbm, ow_hbm, qg, kg, kt, kc, out, wg, fr, acc, qbuf, kv, att, mask, oacc, part_sum, part_lanes,
           fsem, osem, zsend, zrecv, bsend, brecv, hsend, hrecv, gsend, grecv):
    dp, c = lax.axis_index("dp"), lax.axis_index("ctx")
    z, core = c // 2, c % 2
    x, y = dp % NX, dp // NX
    sib = (dp, z * 2 + 1 - core)
    prv, nxt = (dp, (c + NC - 1) % NC), (dp, (c + 1) % NC)

    def zdev(step):
        return (dp, ((z + step + NZ) % NZ) * 2 + core)

    def xydev(i, j):
        return (((y + j + NY) % NY) * NX + (x + i + NX) % NX, c)

    frames = pltpu.make_async_copy(fr_hbm, fr, fsem)
    own = []
    for r, (j, h) in enumerate(ROUNDS):
        cols = pl.ds(h * HD, HD)
        src = ow_hbm.at[:, cols] if j == 3 else pw_hbm.at[j, :, cols]
        own.append(pltpu.make_async_copy(src, wg.at[r, c], osem.at[r]))
    for copy in own:
        copy.start()
    frames.start()

    barrier = pltpu.get_barrier_semaphore()
    greeted = [zdev(1), zdev(-1), prv, nxt]
    greeted += [xydev(i, 0) for i in (-1, 1, 2)] + [xydev(0, j) for j in (-1, 1, 2)]
    for device in greeted:
        pl.semaphore_signal(barrier, inc=1, device_id=device, device_id_type=MESH)
    pl.semaphore_wait(barrier, len(greeted))

    def zcopy(direction, r, owner, hop, sub):
        piece = wg.at[r, owner * 2 + core, pl.ds(sub * HALF, HALF)]
        return pltpu.make_async_remote_copy(
            src_ref=piece, dst_ref=piece, send_sem=zsend, recv_sem=zrecv.at[direction, r, hop, sub],
            device_id=zdev(1 - 2 * direction), device_id_type=MESH,
        )

    def bcopy(r, owner, which):
        piece = wg.at[r, owner * 2 + which]
        return pltpu.make_async_remote_copy(
            src_ref=piece, dst_ref=piece, send_sem=bsend, recv_sem=brecv.at[r, owner],
            device_id=sib, device_id_type=MESH,
        )

    def send_own(r):
        for i in range(2):
            for direction in range(2):
                zcopy(direction, r, z, 0, i ^ direction).start()
        bcopy(r, z, core).start()

    def zat(step):
        return (z + step + NZ) % NZ

    for copy in own:
        copy.wait()
    for r in range(3):
        send_own(r)

    lane_tile = lax.broadcasted_iota(jnp.int32, (QT, KEYS), 1) // TILE + (c - 1) * QT
    row = lax.broadcasted_iota(jnp.int32, (QT, QT), 0)
    col = lax.broadcasted_iota(jnp.int32, (QT, QT), 1)
    for h in range(2):
        counts = jnp.sum(
            jnp.where(row == col, kc[h:h + 1, :].astype(F32), 0.0), axis=1, keepdims=True
        ).astype(jnp.int32)
        listed = jnp.zeros((QT, KEYS), F32)
        for s in range(SLOTS):
            tile = jnp.where(s < counts, kt[h, :, s:s + 1], -1000)
            listed = jnp.where(lane_tile == tile, 1.0, listed)
        for i in range(QT):
            for slot in range(3):
                mask[h, slot, i] = listed[i:i + 1, slot * TOK:(slot + 1) * TOK]

    def project(r, owner, first=False):
        cols = pl.ds(pl.multiple_of(owner * (2 * ROWS), 2 * ROWS), 2 * ROWS)
        weight = wg[r, pl.ds(owner * 2, 2)].reshape(2 * ROWS, HD)
        part = jnp.dot(fr[:, cols], weight, preferred_element_type=F32)
        if first:
            acc[r] = part
        else:
            acc[r] += part

    def normed(r, gain):
        rows = acc[r]
        stat = jnp.mean(rows * rows, axis=-1, keepdims=True)
        return (rows * lax.rsqrt(stat + EPS) * gain).astype(BF16)

    def halo(h, which, side):
        return pltpu.make_async_remote_copy(
            src_ref=kv.at[h, which, 1], dst_ref=kv.at[h, which, 2 - 2 * side], send_sem=hsend,
            recv_sem=hrecv.at[h, which, side], device_id=(dp, (c + NC - 1 + 2 * side) % NC),
            device_id_type=MESH,
        )

    def send_halo(h, which):
        halo(h, which, 1 - core).start()
        halo(h, which, core).start()

    def weigh(h, b, slot):
        rows = pl.ds(pl.multiple_of(b * 128, 128), 128)
        scores = lax.dot_general(
            qbuf[rows, :], kv[h, 0, slot], (((1,), (1,)), ((), ())), preferred_element_type=F32
        )
        live = jnp.concatenate(
            [jnp.broadcast_to(mask[h, slot, b * 2 + i], (TILE, TOK)) for i in range(2)], axis=0
        )
        weights = jnp.where(live > 0.5, jnp.exp2(scores * SCALE), 0.0)
        lanes = sum(weights[:, i * HD:(i + 1) * HD] for i in range(TOK // HD))
        summed = jnp.dot(weights.astype(BF16), kv[h, 1, slot], preferred_element_type=F32)
        return summed, lanes

    def attend_near(h):
        for which in range(2):
            halo(h, which, core).wait_recv()

        def near(b, carry):
            rows = pl.ds(pl.multiple_of(b * 128, 128), 128)
            summed, lanes = weigh(h, b, 1)
            more, more_lanes = weigh(h, b, 2 - 2 * core)
            part_sum[rows, :] = summed + more
            part_lanes[rows, :] = lanes + more_lanes
            return carry

        lax.fori_loop(0, TOK // 128, near, 0)

    def attend_far(h, part):
        if part == 0:
            for which in range(2):
                halo(h, which, 1 - core).wait_recv()

        def far(b, carry):
            rows = pl.ds(pl.multiple_of(b * 128, 128), 128)
            summed, lanes = weigh(h, b, 2 * core)
            total = jnp.sum(part_lanes[rows, :] + lanes, axis=-1, keepdims=True)
            att[h, dp, rows, :] = ((part_sum[rows, :] + summed) / total).astype(BF16)
            return carry

        lax.fori_loop(2 * part, 2 * part + 2, far, 0)
        gather0(h, part)

    def gcopy(h, part, stage, direction, hop, across, along, half, step):
        i, j = (across, along) if part == 0 else (along, across)
        owner = ((y + j + NY) % NY) * NX + (x + i + NX) % NX
        start, size = part * 256, 256
        if half:
            start, size = start + direction * 128, 128
        piece = att.at[h, owner, pl.ds(start, size)]
        target = xydev(step, 0) if (stage == 0) == (part == 0) else xydev(0, step)
        return pltpu.make_async_remote_copy(
            src_ref=piece, dst_ref=piece, send_sem=gsend,
            recv_sem=grecv.at[h, part, stage, direction, hop], device_id=target, device_id_type=MESH,
        )

    OFF = (0, -1, 1, 2)
    PASSED = ((), (0, 1, 2))

    def first_send(h, part):
        for direction in range(2):
            gcopy(h, part, 0, direction, 0, 0, 0, False, 1 - 2 * direction).start()
        gcopy(h, part, 0, 0, 1, 0, 0, False, 2).start()

    def first_wait(h, part, k):
        gcopy(h, part, 0, (0, 0, 1, 0)[k], k // 3, OFF[k], 0, False, 1).wait_recv()

    def second_send(h, part, k):
        for direction in range(2):
            gcopy(h, part, 1 + k, direction, 0, OFF[k], 0, False, 1 - 2 * direction).start()
        if k not in PASSED[h]:
            gcopy(h, part, 1 + k, 0, 1, OFF[k], 0, False, 2).start()

    def second_pass(h, part, k):
        for direction in range(2):
            step = 1 - 2 * direction
            gcopy(h, part, 1 + k, direction, 0, OFF[k], -step, False, step).wait_recv()
            gcopy(h, part, 1 + k, direction, 1, OFF[k], -step, True, step).start()

    def second_wait(h, part, k):
        if k in PASSED[h]:
            for direction in range(2):
                gcopy(h, part, 1 + k, direction, 1, OFF[k], 2, True, 1).wait_recv()
        else:
            for direction in range(2):
                step = 1 - 2 * direction
                gcopy(h, part, 1 + k, direction, 0, OFF[k], -step, False, step).wait_recv()
            gcopy(h, part, 1 + k, 0, 1, OFF[k], 2, False, 1).wait_recv()

    def gather0(h, part):
        first_send(h, part)
        second_send(h, part, 0)

    def gather1(h):
        for k in (1, 2, 3):
            for part in range(2):
                first_wait(h, part, k)
                second_send(h, part, k)
        if 0 in PASSED[h]:
            for part in range(2):
                second_pass(h, part, 0)

    def gather2(h):
        for k in PASSED[h]:
            if k > 0:
                for part in range(2):
                    second_pass(h, part, k)

    def pass_on(r, s):
        if s == 4:
            for direction in range(2):
                zcopy(direction, r, zat(4), 3, direction).wait_recv()
            bcopy(r, zat(4), core).start()
            return
        for i in range(2):
            for direction in range(2):
                sub = i ^ direction
                owner = zat(-s if direction == 0 else s)
                zcopy(direction, r, owner, s - 1, sub).wait_recv()
                if s < 3 or sub == direction:
                    zcopy(direction, r, owner, s, sub).start()
        for step in (-s, s):
            bcopy(r, zat(step), core).start()

    def from_sibling(r, owner):
        bcopy(r, owner, 1 - core).wait_recv()

    def add(r, s, rounds=1):
        owners = {0: 1, 4: 1}.get(s, 2)

        def step(i, carry):
            at = r + i // owners
            owner = zat(s * (2 * (i % owners) - 1))
            from_sibling(at, owner)
            project(at, owner, first=s == 0)
            return carry

        lax.fori_loop(0, rounds * owners, step, 0)

    def finish_keys(g):
        add(3 * g, 4)
        kv[g, 0, 1] = normed(3 * g, kg[g:g + 1, :])
        send_halo(g, 0)
        add(3 * g + 1, 4)
        kv[g, 1, 1] = acc[3 * g + 1].astype(BF16)
        send_halo(g, 1)

    def finish_query(g):
        add(3 * g + 2, 4)
        qbuf[...] = normed(3 * g + 2, qg[g:g + 1, :])

    def mix_hop(s):
        owners = []
        for step in (s,) if s in (0, 4) else (-s, s):
            from_sibling(6, zat(step))
            owners += [zat(step) * 2, zat(step) * 2 + 1]
        left = jnp.concatenate([att[0, owner] for owner in owners], axis=1)
        right = jnp.concatenate([wg[6, owner] for owner in owners], axis=1)
        mixed = lax.dot_general(
            left, right, (((1,), (1,)), ((), ())), preferred_element_type=F32
        )
        if s == 0:
            oacc[...] = mixed
        else:
            oacc[...] += mixed

    def mix(part, k):
        rows = pl.ds(part * 256, 256)
        owners = []
        for j in range(4):
            if part == 0:
                owners.append(j * NX + (x + OFF[k] + NX) % NX)
            else:
                owners.append((y + OFF[k] + NY) % NY * NX + j)
        left = jnp.concatenate([att[1, owner, rows, :] for owner in owners], axis=1)
        right = jnp.concatenate([wg[7, owner] for owner in owners], axis=1)
        mixed = oacc[rows, :] + lax.dot_general(
            left, right, (((1,), (1,)), ((), ())), preferred_element_type=F32
        )
        if k == 3:
            out[rows, :] = mixed.astype(BF16)
        else:
            oacc[rows, :] = mixed

    def pass_all(*steps):
        for r, s in steps:
            pass_on(r, s)

    frames.wait()
    add(0, 0, 3)
    for g in range(2):
        k, v, q, before = 3 * g, 3 * g + 1, 3 * g + 2, 3 * g - 1
        pass_on(k, 1)
        pass_on(v, 1)
        if g == 1:
            send_own(q)
            pass_on(before, 4)
            add(k, 0, 3)
        add(k, 1, 2)
        if g == 1:
            finish_query(0)
            attend_near(0)
        pass_on(k, 2)
        pass_on(v, 2)
        if g == 1:
            attend_far(0, 0)
        pass_on(q, 1)
        if g == 1:
            attend_far(0, 1)
        add(k, 2, 2)
        add(q, 1)
        pass_on(k, 3)
        pass_on(v, 3)
        pass_on(q, 2)
        if g == 0:
            send_own(3)
            send_own(4)
        add(k, 3, 2)
        add(q, 2)
        if g == 1:
            gather1(0)
        pass_on(q, 3)
        pass_on(k, 4)
        pass_on(v, 4)
        if g == 1:
            send_own(6)
        finish_keys(g)
        if g == 1:
            send_own(7)
        add(q, 3)
    pass_on(5, 4)
    finish_query(1)
    attend_near(1)
    attend_far(1, 0)
    attend_far(1, 1)
    pass_all((6, 1), (7, 1), (6, 2), (7, 2))
    gather1(1)
    pass_all((6, 3), (7, 3))
    for k in range(4):
        for part in range(2):
            second_wait(0, part, k)
    for s in range(4):
        mix_hop(s)
    pass_all((6, 4), (7, 4))
    gather2(1)
    mix_hop(4)
    for owner in range(NZ):
        from_sibling(7, owner)
    for k in range(4):
        for part in range(2):
            second_wait(1, part, k)
            mix(part, k)

    for sent, sem in (
        (wg.at[pl.ds(0, 7), pl.ds(0, 8)], zsend),
        (wg.at[pl.ds(0, 4)], bsend),
        (kv.at[:, :, pl.ds(0, 2)], hsend),
        (att.at[:, pl.ds(0, 15)], gsend),
    ):
        pltpu.make_async_copy(sent, sent, sem).wait()


def body(frames, proj_weight, out_weight, query_gain, key_gain, key_tiles, key_counts):
    anywhere = pl.BlockSpec(memory_space=pl.ANY)
    vmem = pl.BlockSpec(memory_space=pltpu.VMEM)
    dma = pltpu.SemaphoreType.DMA
    return pl.pallas_call(
        kernel,
        out_shape=jax.ShapeDtypeStruct((TOK, ROWS), BF16),
        in_specs=[anywhere] * 3 + [vmem] * 4,
        out_specs=vmem,
        scratch_shapes=[
            pltpu.VMEM((8, NC, ROWS, HD), BF16),
            pltpu.VMEM((TOK, D), BF16),
            pltpu.VMEM((6, TOK, HD), F32),
            pltpu.VMEM((TOK, HD), BF16),
            pltpu.VMEM((2, 2, 3, TOK, HD), BF16),
            pltpu.VMEM((2, 16, TOK, HD), BF16),
            pltpu.VMEM((2, 3, QT, 1, TOK), F32),
            pltpu.VMEM((TOK, ROWS), F32),
            pltpu.VMEM((TOK, HD), F32),
            pltpu.VMEM((TOK, HD), F32),
            dma, dma((8,)),
            dma, dma((2, 8, 4, 2)),
            dma, dma((8, 8)),
            dma, dma((2, 2, 2)),
            dma, dma((2, 2, 5, 2, 2)),
        ],
        compiler_params=pltpu.CompilerParams(
            collective_id=0, has_side_effects=True, vmem_limit_bytes=56 * 2**20
        ),
        cost_estimate=pl.CostEstimate(
            flops=8 * 10**9, bytes_accessed=8 * 10**6, transcendentals=2 * 10**6
        ),
        name="layer",
    )(
        frames, proj_weight, out_weight, query_gain.reshape(2, HD), key_gain.reshape(2, HD),
        key_tiles, key_counts,
    )


def solution(mesh):
    placed = (
        P("ctx", None),
        P(None, "ctx", "dp"),
        P("dp", "ctx"),
        P("dp"),
        P("dp"),
        P("dp", "ctx", None),
        P("dp", "ctx"),
    )
    return jax.shard_map(
        body, mesh=mesh, in_specs=placed, out_specs=P("ctx", "dp"), check_vma=False
    )
```

```python
import math

import jax
import jax.numpy as jnp
from jax import lax
from jax.experimental import pallas as pl
from jax.experimental.pallas import tpu as pltpu
from jax.sharding import PartitionSpec as P

MESH = pl.DeviceIdType.MESH
F32, BF16 = jnp.float32, jnp.bfloat16

D = 6144
HD = 128
TILE = 64
TOK = 512
QT = 8
SLOTS = 18
NZ = 8
NX = 4
NY = 4
NC = 16
ROWS = 384
HALF = 192
KEYS = 3 * TOK
EPS = 1e-06
SCALE = math.log2(math.e) / math.sqrt(HD)

ROUNDS = ((1, 0), (2, 0), (0, 0), (1, 1), (2, 1), (0, 1), (3, 0), (3, 1))


def kernel(fr_hbm, pw_hbm, ow_hbm, qg, kg, kt, kc, out, wg, fr, acc, qbuf, kv, att, mask, oacc, part_sum, part_lanes,
           fsem, osem, zsend, zrecv, bsend, brecv, hsend, hrecv, gsend, grecv):
    dp, c = lax.axis_index("dp"), lax.axis_index("ctx")
    z, core = c // 2, c % 2
    x, y = dp % NX, dp // NX
    sib = (dp, z * 2 + 1 - core)
    prv, nxt = (dp, (c + NC - 1) % NC), (dp, (c + 1) % NC)

    def zdev(step):
        return (dp, ((z + step + NZ) % NZ) * 2 + core)

    def xydev(i, j):
        return (((y + j + NY) % NY) * NX + (x + i + NX) % NX, c)

    frames = pltpu.make_async_copy(fr_hbm, fr, fsem)
    own = []
    for r, (j, h) in enumerate(ROUNDS):
        cols = pl.ds(h * HD, HD)
        src = ow_hbm.at[:, cols] if j == 3 else pw_hbm.at[j, :, cols]
        own.append(pltpu.make_async_copy(src, wg.at[r, c], osem.at[r]))
    for copy in own:
        copy.start()
    frames.start()

    barrier = pltpu.get_barrier_semaphore()
    greeted = [zdev(1), zdev(-1), prv, nxt]
    greeted += [xydev(i, 0) for i in (-1, 1, 2)] + [xydev(0, j) for j in (-1, 1, 2)]
    for device in greeted:
        pl.semaphore_signal(barrier, inc=1, device_id=device, device_id_type=MESH)
    pl.semaphore_wait(barrier, len(greeted))

    def zcopy(direction, r, owner, hop, sub):
        piece = wg.at[r, owner * 2 + core, pl.ds(sub * HALF, HALF)]
        return pltpu.make_async_remote_copy(
            src_ref=piece, dst_ref=piece, send_sem=zsend, recv_sem=zrecv.at[direction, r, hop, sub],
            device_id=zdev(1 - 2 * direction), device_id_type=MESH,
        )

    def bcopy(r, owner, which):
        piece = wg.at[r, owner * 2 + which]
        return pltpu.make_async_remote_copy(
            src_ref=piece, dst_ref=piece, send_sem=bsend, recv_sem=brecv.at[r, owner],
            device_id=sib, device_id_type=MESH,
        )

    def send_own(r):
        for i in range(2):
            for direction in range(2):
                zcopy(direction, r, z, 0, i ^ direction).start()
        bcopy(r, z, core).start()

    def zat(step):
        return (z + step + NZ) % NZ

    for copy in own:
        copy.wait()
    for r in range(3):
        send_own(r)

    lane_tile = lax.broadcasted_iota(jnp.int32, (QT, KEYS), 1) // TILE + (c - 1) * QT
    row = lax.broadcasted_iota(jnp.int32, (QT, QT), 0)
    col = lax.broadcasted_iota(jnp.int32, (QT, QT), 1)
    for h in range(2):
        counts = jnp.sum(
            jnp.where(row == col, kc[h:h + 1, :].astype(F32), 0.0), axis=1, keepdims=True
        ).astype(jnp.int32)
        listed = jnp.zeros((QT, KEYS), F32)
        for s in range(SLOTS):
            tile = jnp.where(s < counts, kt[h, :, s:s + 1], -1000)
            listed = jnp.where(lane_tile == tile, 1.0, listed)
        for i in range(QT):
            for slot in range(3):
                mask[h, slot, i] = listed[i:i + 1, slot * TOK:(slot + 1) * TOK]

    def project(r, owner, first=False):
        cols = pl.ds(pl.multiple_of(owner * (2 * ROWS), 2 * ROWS), 2 * ROWS)
        weight = wg[r, pl.ds(owner * 2, 2)].reshape(2 * ROWS, HD)
        part = jnp.dot(fr[:, cols], weight, preferred_element_type=F32)
        if first:
            acc[r] = part
        else:
            acc[r] += part

    def normed(r, gain):
        rows = acc[r]
        stat = jnp.mean(rows * rows, axis=-1, keepdims=True)
        return (rows * lax.rsqrt(stat + EPS) * gain).astype(BF16)

    def halo(h, which, side):
        return pltpu.make_async_remote_copy(
            src_ref=kv.at[h, which, 1], dst_ref=kv.at[h, which, 2 - 2 * side], send_sem=hsend,
            recv_sem=hrecv.at[h, which, side], device_id=(dp, (c + NC - 1 + 2 * side) % NC),
            device_id_type=MESH,
        )

    def send_halo(h, which):
        halo(h, which, 1 - core).start()
        halo(h, which, core).start()

    def weigh(h, b, slot):
        rows = pl.ds(pl.multiple_of(b * 128, 128), 128)
        scores = lax.dot_general(
            qbuf[rows, :], kv[h, 0, slot], (((1,), (1,)), ((), ())), preferred_element_type=F32
        )
        live = jnp.concatenate(
            [jnp.broadcast_to(mask[h, slot, b * 2 + i], (TILE, TOK)) for i in range(2)], axis=0
        )
        weights = jnp.where(live > 0.5, jnp.exp2(scores * SCALE), 0.0)
        lanes = sum(weights[:, i * HD:(i + 1) * HD] for i in range(TOK // HD))
        summed = jnp.dot(weights.astype(BF16), kv[h, 1, slot], preferred_element_type=F32)
        return summed, lanes

    def attend_near(h):
        for which in range(2):
            halo(h, which, core).wait_recv()

        def near(b, carry):
            rows = pl.ds(pl.multiple_of(b * 128, 128), 128)
            summed, lanes = weigh(h, b, 1)
            more, more_lanes = weigh(h, b, 2 - 2 * core)
            part_sum[rows, :] = summed + more
            part_lanes[rows, :] = lanes + more_lanes
            return carry

        lax.fori_loop(0, TOK // 128, near, 0)

    def attend_far(h, part):
        if part == 0:
            for which in range(2):
                halo(h, which, 1 - core).wait_recv()

        def far(b, carry):
            rows = pl.ds(pl.multiple_of(b * 128, 128), 128)
            summed, lanes = weigh(h, b, 2 * core)
            total = jnp.sum(part_lanes[rows, :] + lanes, axis=-1, keepdims=True)
            att[h, dp, rows, :] = ((part_sum[rows, :] + summed) / total).astype(BF16)
            return carry

        lax.fori_loop(2 * part, 2 * part + 2, far, 0)
        gather0(h, part)

    def gcopy(h, part, stage, direction, hop, across, along, half, step):
        i, j = (across, along) if part == 0 else (along, across)
        owner = ((y + j + NY) % NY) * NX + (x + i + NX) % NX
        start, size = part * 256, 256
        if half:
            start, size = start + direction * 128, 128
        piece = att.at[h, owner, pl.ds(start, size)]
        target = xydev(step, 0) if (stage == 0) == (part == 0) else xydev(0, step)
        return pltpu.make_async_remote_copy(
            src_ref=piece, dst_ref=piece, send_sem=gsend,
            recv_sem=grecv.at[h, part, stage, direction, hop], device_id=target, device_id_type=MESH,
        )

    OFF = (0, -1, 1, 2)
    PASSED = ((), (0, 1, 2))

    def first_send(h, part):
        for direction in range(2):
            gcopy(h, part, 0, direction, 0, 0, 0, False, 1 - 2 * direction).start()
        gcopy(h, part, 0, 0, 1, 0, 0, False, 2).start()

    def first_wait(h, part, k):
        gcopy(h, part, 0, (0, 0, 1, 0)[k], k // 3, OFF[k], 0, False, 1).wait_recv()

    def second_send(h, part, k):
        for direction in range(2):
            gcopy(h, part, 1 + k, direction, 0, OFF[k], 0, False, 1 - 2 * direction).start()
        if k not in PASSED[h]:
            gcopy(h, part, 1 + k, 0, 1, OFF[k], 0, False, 2).start()

    def second_pass(h, part, k):
        for direction in range(2):
            step = 1 - 2 * direction
            gcopy(h, part, 1 + k, direction, 0, OFF[k], -step, False, step).wait_recv()
            gcopy(h, part, 1 + k, direction, 1, OFF[k], -step, True, step).start()

    def second_wait(h, part, k):
        if k in PASSED[h]:
            for direction in range(2):
                gcopy(h, part, 1 + k, direction, 1, OFF[k], 2, True, 1).wait_recv()
        else:
            for direction in range(2):
                step = 1 - 2 * direction
                gcopy(h, part, 1 + k, direction, 0, OFF[k], -step, False, step).wait_recv()
            gcopy(h, part, 1 + k, 0, 1, OFF[k], 2, False, 1).wait_recv()

    def gather0(h, part):
        first_send(h, part)
        if part == 1:
            second_send(h, 0, 0)
            second_send(h, 1, 0)

    def gather1(h):
        for k in (1, 2, 3):
            for part in range(2):
                first_wait(h, part, k)
                second_send(h, part, k)
        if 0 in PASSED[h]:
            for part in range(2):
                second_pass(h, part, 0)

    def gather2(h):
        for k in PASSED[h]:
            if k > 0:
                for part in range(2):
                    second_pass(h, part, k)

    def pass_on(r, s):
        if s == 4:
            for direction in range(2):
                zcopy(direction, r, zat(4), 3, direction).wait_recv()
            bcopy(r, zat(4), core).start()
            return
        for i in range(2):
            for direction in range(2):
                sub = i ^ direction
                owner = zat(-s if direction == 0 else s)
                zcopy(direction, r, owner, s - 1, sub).wait_recv()
                if s < 3 or sub == direction:
                    zcopy(direction, r, owner, s, sub).start()
        for step in (-s, s):
            bcopy(r, zat(step), core).start()

    def from_sibling(r, owner):
        bcopy(r, owner, 1 - core).wait_recv()

    def add(r, s, rounds=1):
        owners = {0: 1, 4: 1}.get(s, 2)

        def step(i, carry):
            at = r + i // owners
            owner = zat(s * (2 * (i % owners) - 1))
            from_sibling(at, owner)
            project(at, owner, first=s == 0)
            return carry

        lax.fori_loop(0, rounds * owners, step, 0)

    def finish_keys(g):
        add(3 * g, 4)
        kv[g, 0, 1] = normed(3 * g, kg[g:g + 1, :])
        send_halo(g, 0)
        add(3 * g + 1, 4)
        kv[g, 1, 1] = acc[3 * g + 1].astype(BF16)
        send_halo(g, 1)

    def finish_query(g):
        add(3 * g + 2, 4)
        qbuf[...] = normed(3 * g + 2, qg[g:g + 1, :])

    def mix_hop(s):
        owners = []
        for step in (s,) if s in (0, 4) else (-s, s):
            from_sibling(6, zat(step))
            owners += [zat(step) * 2, zat(step) * 2 + 1]
        left = jnp.concatenate([att[0, owner] for owner in owners], axis=1)
        right = jnp.concatenate([wg[6, owner] for owner in owners], axis=1)
        mixed = lax.dot_general(
            left, right, (((1,), (1,)), ((), ())), preferred_element_type=F32
        )
        if s == 0:
            oacc[...] = mixed
        else:
            oacc[...] += mixed

    def mix(part, k):
        rows = pl.ds(part * 256, 256)
        owners = []
        for j in range(4):
            if part == 0:
                owners.append(j * NX + (x + OFF[k] + NX) % NX)
            else:
                owners.append((y + OFF[k] + NY) % NY * NX + j)
        left = jnp.concatenate([att[1, owner, rows, :] for owner in owners], axis=1)
        right = jnp.concatenate([wg[7, owner] for owner in owners], axis=1)
        mixed = oacc[rows, :] + lax.dot_general(
            left, right, (((1,), (1,)), ((), ())), preferred_element_type=F32
        )
        if k == 3:
            out[rows, :] = mixed.astype(BF16)
        else:
            oacc[rows, :] = mixed

    def pass_all(*steps):
        for r, s in steps:
            pass_on(r, s)

    frames.wait()
    add(0, 0, 3)
    for g in range(2):
        k, v, q, before = 3 * g, 3 * g + 1, 3 * g + 2, 3 * g - 1
        pass_on(k, 1)
        pass_on(v, 1)
        if g == 1:
            send_own(q)
            pass_on(before, 4)
            add(k, 0, 3)
        add(k, 1, 2)
        if g == 1:
            finish_query(0)
            attend_near(0)
        pass_on(k, 2)
        pass_on(v, 2)
        if g == 1:
            attend_far(0, 0)
        pass_on(q, 1)
        if g == 1:
            attend_far(0, 1)
        add(k, 2, 2)
        add(q, 1)
        pass_on(k, 3)
        pass_on(v, 3)
        pass_on(q, 2)
        if g == 0:
            send_own(3)
            send_own(4)
        add(k, 3, 2)
        add(q, 2)
        if g == 1:
            gather1(0)
        pass_on(q, 3)
        pass_on(k, 4)
        pass_on(v, 4)
        if g == 1:
            send_own(6)
        finish_keys(g)
        if g == 1:
            send_own(7)
        add(q, 3)
    pass_on(5, 4)
    finish_query(1)
    attend_near(1)
    attend_far(1, 0)
    attend_far(1, 1)
    pass_all((6, 1), (7, 1), (6, 2), (7, 2))
    gather1(1)
    pass_all((6, 3), (7, 3))
    for k in range(4):
        for part in range(2):
            second_wait(0, part, k)
    for s in range(4):
        mix_hop(s)
    pass_all((6, 4), (7, 4))
    gather2(1)
    mix_hop(4)
    for owner in range(NZ):
        from_sibling(7, owner)
    for k in range(4):
        for part in range(2):
            second_wait(1, part, k)
            mix(part, k)

    for sent, sem in (
        (wg.at[pl.ds(0, 7), pl.ds(0, 8)], zsend),
        (wg.at[pl.ds(0, 4)], bsend),
        (kv.at[:, :, pl.ds(0, 2)], hsend),
        (att.at[:, pl.ds(0, 15)], gsend),
    ):
        pltpu.make_async_copy(sent, sent, sem).wait()


def body(frames, proj_weight, out_weight, query_gain, key_gain, key_tiles, key_counts):
    anywhere = pl.BlockSpec(memory_space=pl.ANY)
    vmem = pl.BlockSpec(memory_space=pltpu.VMEM)
    dma = pltpu.SemaphoreType.DMA
    return pl.pallas_call(
        kernel,
        out_shape=jax.ShapeDtypeStruct((TOK, ROWS), BF16),
        in_specs=[anywhere] * 3 + [vmem] * 4,
        out_specs=vmem,
        scratch_shapes=[
            pltpu.VMEM((8, NC, ROWS, HD), BF16),
            pltpu.VMEM((TOK, D), BF16),
            pltpu.VMEM((6, TOK, HD), F32),
            pltpu.VMEM((TOK, HD), BF16),
            pltpu.VMEM((2, 2, 3, TOK, HD), BF16),
            pltpu.VMEM((2, 16, TOK, HD), BF16),
            pltpu.VMEM((2, 3, QT, 1, TOK), F32),
            pltpu.VMEM((TOK, ROWS), F32),
            pltpu.VMEM((TOK, HD), F32),
            pltpu.VMEM((TOK, HD), F32),
            dma, dma((8,)),
            dma, dma((2, 8, 4, 2)),
            dma, dma((8, 8)),
            dma, dma((2, 2, 2)),
            dma, dma((2, 2, 5, 2, 2)),
        ],
        compiler_params=pltpu.CompilerParams(
            collective_id=0, has_side_effects=True, vmem_limit_bytes=56 * 2**20
        ),
        cost_estimate=pl.CostEstimate(
            flops=8 * 10**9, bytes_accessed=8 * 10**6, transcendentals=2 * 10**6
        ),
        name="layer",
    )(
        frames, proj_weight, out_weight, query_gain.reshape(2, HD), key_gain.reshape(2, HD),
        key_tiles, key_counts,
    )


def solution(mesh):
    placed = (
        P("ctx", None),
        P(None, "ctx", "dp"),
        P("dp", "ctx"),
        P("dp"),
        P("dp"),
        P("dp", "ctx", None),
        P("dp", "ctx"),
    )
    return jax.shard_map(
        body, mesh=mesh, in_specs=placed, out_specs=P("ctx", "dp"), check_vma=False
    )
```
